512 devices in a mesh: row: 16 (over y, z_hi, core), col: 32 (over z_lo, x).
Axes of the slice: x: 4, y: 4, z: 16 (z_hi: 2, z_lo: 8; z = z_hi * 8 + z_lo), core: 2. Of those that a mesh axis runs over, the one named last changes fastest.
Arguments:
- grad_out: bfloat16 [512, 16384], P('row', 'col'), may hold values from -6 to 6
- gate_pre: bfloat16 [512, 26624], P('col', 'row'), may hold values from -6 to 6
- up_pre: bfloat16 [512, 26624], P('col', 'row'), may hold values from -6 to 6
- weight_values: bfloat16 [26624, 16384], P('row', 'col'), may hold values from -0.0390625 to 0.0390625
- weight_scales: float32 [512, 26624], P('col', 'row'), may hold values from 0.25 to 4, as said below
Outputs:
- weight_grad: bfloat16 [26624, 16384], P('row', 'col')
- gate_grad: bfloat16 [512, 26624], P('col', 'row')
- up_grad: bfloat16 [512, 26624], P('col', 'row')
The draws below stay inside these ranges and needn't reach their ends.
Inputs may be any that keep to these rules, and one draw needn't show every extreme that they name: `weight_scales`: every scale is a power of two.
All inputs are finite; a program needn't handle non-finite values.
Results may differ from the reference program's by a relative error of at most 0.006.
Values may be sent and summed in bfloat16 or wider, within the bound.
No kernel may reach another device: no remote copies, remote signals or barrier semaphores. Data moves between devices by JAX's collectives and lax.ppermute only.
A program may use at most 64 MiB of HBM per device.

```python
import jax
import jax.numpy as jnp
from jax import lax

D = 16384
FF = 26624
BLOCK = 32
TOKENS = 512
N_ROW = 16


def draw_weight_scales(key, part):
    key = jax.random.fold_in(key, 11)
    levels = jnp.array([0.25, 0.5, 1.0, 2.0, 4.0], jnp.float32)
    picks = jax.random.randint(key, (D // BLOCK, FF), 0, 5)
    return jnp.take(levels, picks).astype(jnp.float32)


def block_scale(stream_key, shape, pieces, least, largest):
    factor_of = 1.0
    for dim, shards_of in pieces:
        draws = jax.random.uniform(jax.random.fold_in(jax.random.fold_in(stream_key, 6), dim), (shards_of,), jnp.float32, least / len(pieces), largest / len(pieces))
        factor_of = factor_of * jnp.repeat(jnp.exp(draws), shape[dim] // shards_of).reshape((-1,) + (1,) * (len(shape) - 1 - dim))
    return factor_of


def scatter_about(own_key, shape, scale, limit, cuts=(), kind=jnp.bfloat16):
    drawn = jax.random.normal(own_key, shape, jnp.float32) * scale
    if len(cuts) > 0:
        drawn = block_scale(own_key, shape, cuts, -0.22, 0.18) * drawn
    return jnp.clip(drawn, min=-limit, max=limit).astype(kind)


def setup_inputs(seed: int = 0) -> dict:
    key_of = jax.random.split(jax.random.key(seed), 6)
    grad_out = scatter_about(key_of[0], (TOKENS, D), 1.0, 6.0, ((0, 16), (1, 32)))
    gate_pre = scatter_about(key_of[1], (TOKENS, FF), 1.0, 6.0, ((0, 32), (1, 16)))
    up_pre = scatter_about(key_of[2], (TOKENS, FF), 1.0, 6.0, ((0, 32), (1, 16)))
    weight_values = scatter_about(key_of[3], (FF, D), FF ** -0.5, 0.0390625, ((0, 16), (1, 32)))
    weight_scales = draw_weight_scales(jax.random.fold_in(key_of[5], 71), 0)
    return dict(grad_out=grad_out, gate_pre=gate_pre, up_pre=up_pre, weight_values=weight_values, weight_scales=weight_scales)


def reference(grad_out, gate_pre, up_pre, weight_values, weight_scales):
    gate_f = gate_pre.astype(jnp.float32)
    up_f = up_pre.astype(jnp.float32)
    sig = jax.nn.sigmoid(gate_f)
    act = gate_f * sig
    hidden = (act * up_f).astype(jnp.bfloat16)
    width = FF // N_ROW
    values_parts = weight_values.reshape(N_ROW, width, D)
    scale_parts = jnp.transpose(weight_scales).reshape(N_ROW, width, D // BLOCK)
    hidden_parts = jnp.transpose(hidden.reshape(TOKENS, N_ROW, width), (1, 0, 2))

    def one_block(items):
        values, scales, hidden_block = items
        weight = (values.astype(jnp.float32) * jnp.repeat(scales, BLOCK, axis=1)).astype(jnp.bfloat16)
        grad_block = lax.dot_general(grad_out, weight, (((1,), (1,)), ((), ())), preferred_element_type=jnp.float32)
        wgrad_block = lax.dot_general(hidden_block, grad_out, (((0,), (0,)), ((), ())), preferred_element_type=jnp.float32)
        return grad_block, wgrad_block.astype(jnp.bfloat16)

    grad_parts, wgrad_parts = lax.map(one_block, (values_parts, scale_parts, hidden_parts))
    hidden_grad = jnp.transpose(grad_parts, (1, 0, 2)).reshape(TOKENS, FF)
    weight_grad = wgrad_parts.reshape(FF, D)
    gate_grad = (hidden_grad * up_f * sig * (1.0 + gate_f * (1.0 - sig))).astype(jnp.bfloat16)
    up_grad = (hidden_grad * act).astype(jnp.bfloat16)
    return (weight_grad, gate_grad, up_grad)
```

```python
import jax
import jax.numpy as jnp
from jax import lax
from jax.sharding import Mesh, PartitionSpec as P

BLOCK = 32


def exchange(parts, axes):
    return lax.all_to_all(parts, axes, split_axis=0, concat_axis=0)


def gather(block, axes, count):
    return exchange(jnp.broadcast_to(block[None], (count,) + block.shape), axes)


def per_device(grad_out, gate_pre, up_pre, weight_values, weight_scales):
    units = gate_pre.shape[1]
    width = grad_out.shape[1]
    gate_f = gate_pre.astype(jnp.float32)
    up_f = up_pre.astype(jnp.float32)
    sig = jax.nn.sigmoid(gate_f)
    act = gate_f * sig
    hidden = (act * up_f).astype(jnp.bfloat16)

    other = lax.ppermute(grad_out, "zh", [(0, 1), (1, 0)])
    upper = lax.axis_index("zh") == 1
    pair = jnp.where(upper, jnp.stack([other, grad_out]), jnp.stack([grad_out, other]))
    grads = gather(pair, ("y", "core"), 8)
    grads = grads.reshape(4, 2, 2, 2, 16, width).transpose(1, 3, 0, 2, 4, 5).reshape(512, width)

    z_hidden = gather(hidden, "z", 8).reshape(128, units)
    all_hidden = gather(z_hidden, "x", 4).reshape(512, units)

    scale_rows = jnp.repeat(weight_scales, BLOCK, axis=0)
    weight = (weight_values.astype(jnp.float32) * jnp.transpose(scale_rows)).astype(jnp.bfloat16)
    partial = lax.dot_general(
        grads, weight, (((1,), (1,)), ((), ())), preferred_element_type=jnp.float32
    ).astype(jnp.bfloat16)
    over_x = exchange(partial.reshape(4, 128, units), "x")
    over_x = over_x.astype(jnp.float32).sum(0).astype(jnp.bfloat16)
    over_z = exchange(over_x.reshape(8, 16, units), "z")
    hidden_grad = over_z.astype(jnp.float32).sum(0)

    weight_grad = lax.dot_general(
        all_hidden, grads, (((0,), (0,)), ((), ())), preferred_element_type=jnp.float32
    ).astype(jnp.bfloat16)
    gate_grad = (hidden_grad * up_f * sig * (1.0 + gate_f * (1.0 - sig))).astype(jnp.bfloat16)
    up_grad = (hidden_grad * act).astype(jnp.bfloat16)
    return (weight_grad, gate_grad, up_grad)


def solution(mesh):
    fine = Mesh(mesh.devices.reshape(4, 2, 2, 8, 4), ("y", "zh", "core", "z", "x"))
    row, col = ("y", "zh", "core"), ("z", "x")
    placed = (P(row, col), P(col, row), P(col, row), P(row, col), P(col, row))
    return jax.shard_map(
        per_device,
        mesh=fine,
        in_specs=placed,
        out_specs=(P(row, col), P(col, row), P(col, row)),
        check_vma=False,
    )
```

```python
import jax
import jax.numpy as jnp
from jax import lax
from jax.sharding import Mesh, PartitionSpec as P

BLOCK = 32


def exchange(parts, axes):
    return lax.all_to_all(parts, axes, split_axis=0, concat_axis=0)


def swap(block, axis, size, stride):
    return lax.ppermute(block, axis, [(i, i ^ stride) for i in range(size)])


def shift(block, k):
    return lax.ppermute(block, "x", [(i, (i + k) % 4) for i in range(4)])


def in_order(mine, other, upper, axis):
    return jnp.where(upper, jnp.stack([other, mine], axis), jnp.stack([mine, other], axis))


def per_device(grad_out, gate_pre, up_pre, weight_values, weight_scales):
    units = gate_pre.shape[1]
    width = grad_out.shape[1]
    gate_f = gate_pre.astype(jnp.float32)
    up_f = up_pre.astype(jnp.float32)
    sig = jax.nn.sigmoid(gate_f)
    act = gate_f * sig
    hidden = (act * up_f).astype(jnp.bfloat16)
    zb, x = lax.axis_index("zb"), lax.axis_index("x")

    part = exchange(jnp.broadcast_to(hidden[None], (4,) + hidden.shape), "za")
    pair = in_order(grad_out, swap(grad_out, "zh", 2, 1), lax.axis_index("zh") == 1, 0)
    spread = (jnp.arange(width)[None] // BLOCK == jnp.arange(width // BLOCK)[:, None]).astype(jnp.float32)
    scale = lax.dot_general(weight_scales, spread, (((0,), (0,)), ((), ())), preferred_element_type=jnp.float32)
    weight = (weight_values.astype(jnp.float32) * scale).astype(jnp.bfloat16)
    pair, part, weight = lax.optimization_barrier((pair, part, weight))

    mine = in_order(part, swap(part, "zb", 2, 1), zb == 1, 1).reshape(128, units)
    grads = exchange(jnp.broadcast_to(pair[None], (8,) + pair.shape), ("y", "core"))
    grads = grads.reshape(4, 2, 2, 2, 16, width)
    by_part = grads.transpose(2, 1, 3, 0, 4, 5).reshape(512, width)
    by_x = grads.transpose(1, 3, 0, 2, 4, 5).reshape(4, 128, width)
    partial = lax.dot_general(
        by_part, weight, (((1,), (1,)), ((), ())), preferred_element_type=jnp.float32
    ).astype(jnp.bfloat16)
    partial, mine = lax.optimization_barrier((partial, mine))

    over_x = exchange(partial.reshape(8, 64, units), ("zb", "x"))
    next_x = shift(mine, 3)
    last_x = shift(mine, 1)
    far_x = shift(mine, 2)
    over_x = over_x.astype(jnp.float32).sum(0).astype(jnp.bfloat16)
    over_z = exchange(over_x.reshape(4, 16, units), "za")
    hidden_grad = over_z.astype(jnp.float32).sum(0)

    all_hidden = jnp.concatenate([mine, next_x, far_x, last_x])
    rolled = lax.dynamic_slice_in_dim(jnp.concatenate([by_x, by_x]), x, 4).reshape(512, width)
    weight_grad = lax.dot_general(
        all_hidden, rolled, (((0,), (0,)), ((), ())), preferred_element_type=jnp.float32
    ).astype(jnp.bfloat16)
    gate_grad = (hidden_grad * up_f * sig * (1.0 + gate_f * (1.0 - sig))).astype(jnp.bfloat16)
    up_grad = (hidden_grad * act).astype(jnp.bfloat16)
    return (weight_grad, gate_grad, up_grad)


def solution(mesh):
    fine = Mesh(mesh.devices.reshape(4, 2, 2, 4, 2, 4), ("y", "zh", "core", "za", "zb", "x"))
    row, col = ("y", "zh", "core"), ("za", "zb", "x")
    placed = (P(row, col), P(col, row), P(col, row), P(row, col), P(col, row))
    return jax.shard_map(
        per_device,
        mesh=fine,
        in_specs=placed,
        out_specs=(P(row, col), P(col, row), P(col, row)),
        check_vma=False,
    )
```

```python
import jax
import jax.numpy as jnp
from jax import lax
from jax.sharding import Mesh, PartitionSpec as P

BLOCK = 32


def exchange(parts, axes):
    return lax.all_to_all(parts, axes, split_axis=0, concat_axis=0)


def swap(block, axis, size, stride):
    return lax.ppermute(block, axis, [(i, i ^ stride) for i in range(size)])


def shift(block, k):
    return lax.ppermute(block, "x", [(i, (i + k) % 4) for i in range(4)])


def in_order(mine, other, upper, axis):
    return jnp.where(upper, jnp.stack([other, mine], axis), jnp.stack([mine, other], axis))


def per_device(grad_out, gate_pre, up_pre, weight_values, weight_scales):
    units = gate_pre.shape[1]
    width = grad_out.shape[1]
    gate_f = gate_pre.astype(jnp.float32)
    up_f = up_pre.astype(jnp.float32)
    sig = jax.nn.sigmoid(gate_f)
    act = gate_f * sig
    hidden = (act * up_f).astype(jnp.bfloat16)
    zb, x = lax.axis_index("zb"), lax.axis_index("x")

    part = exchange(jnp.broadcast_to(hidden[None], (4,) + hidden.shape), "za")
    pair = in_order(grad_out, swap(grad_out, "zh", 2, 1), lax.axis_index("zh") == 1, 0)
    spread = (jnp.arange(width)[None] // BLOCK == jnp.arange(width // BLOCK)[:, None]).astype(jnp.float32)
    scale = lax.dot_general(weight_scales, spread, (((0,), (0,)), ((), ())), preferred_element_type=jnp.float32)
    weight = (weight_values.astype(jnp.float32) * scale).astype(jnp.bfloat16)
    pair, part, weight = lax.optimization_barrier((pair, part, weight))

    mine = in_order(part, swap(part, "zb", 2, 1), zb == 1, 1).reshape(128, units)
    grads = exchange(jnp.broadcast_to(pair[None], (8,) + pair.shape), ("y", "core"))
    grads = grads.reshape(4, 2, 2, 2, 16, width)
    by_part = grads.transpose(1, 3, 2, 0, 4, 5).reshape(512, width)
    by_x = grads.transpose(1, 3, 0, 2, 4, 5).reshape(4, 128, width)
    partial = lax.dot_general(
        by_part, weight, (((1,), (1,)), ((), ())), preferred_element_type=jnp.float32
    ).astype(jnp.bfloat16)
    partial, mine = lax.optimization_barrier((partial, mine))

    over_x = exchange(partial.reshape(8, 64, units), ("x", "zb"))
    next_x = shift(mine, 3)
    last_x = shift(mine, 1)
    far_x = shift(mine, 2)
    over_x = over_x.astype(jnp.float32).sum(0).astype(jnp.bfloat16)
    over_z = exchange(over_x.reshape(4, 16, units), "za")
    hidden_grad = over_z.astype(jnp.float32).sum(0)

    all_hidden = jnp.concatenate([mine, next_x, far_x, last_x])
    rolled = lax.dynamic_slice_in_dim(jnp.concatenate([by_x, by_x]), x, 4).reshape(512, width)
    weight_grad = lax.dot_general(
        all_hidden, rolled, (((0,), (0,)), ((), ())), preferred_element_type=jnp.float32
    ).astype(jnp.bfloat16)
    gate_grad = (hidden_grad * up_f * sig * (1.0 + gate_f * (1.0 - sig))).astype(jnp.bfloat16)
    up_grad = (hidden_grad * act).astype(jnp.bfloat16)
    return (weight_grad, gate_grad, up_grad)


def solution(mesh):
    fine = Mesh(mesh.devices.reshape(4, 2, 2, 4, 2, 4), ("y", "zh", "core", "za", "zb", "x"))
    row, col = ("y", "zh", "core"), ("za", "zb", "x")
    placed = (P(row, col), P(col, row), P(col, row), P(row, col), P(col, row))
    return jax.shard_map(
        per_device,
        mesh=fine,
        in_specs=placed,
        out_specs=(P(row, col), P(col, row), P(col, row)),
        check_vma=False,
    )
```

```python
import jax
import jax.numpy as jnp
from jax import lax
from jax.sharding import Mesh, PartitionSpec as P

BLOCK = 32


def exchange(parts, axes):
    return lax.all_to_all(parts, axes, split_axis=0, concat_axis=0)


def swap(block, axis, size, stride):
    return lax.ppermute(block, axis, [(i, i ^ stride) for i in range(size)])


def shift(block, k):
    return lax.ppermute(block, "x", [(i, (i + k) % 4) for i in range(4)])


def in_order(mine, other, upper, axis):
    return jnp.where(upper, jnp.stack([other, mine], axis), jnp.stack([mine, other], axis))


def per_device(grad_out, gate_pre, up_pre, weight_values, weight_scales):
    units = gate_pre.shape[1]
    width = grad_out.shape[1]
    gate_f = gate_pre.astype(jnp.float32)
    up_f = up_pre.astype(jnp.float32)
    sig = jax.nn.sigmoid(gate_f)
    act = gate_f * sig
    hidden = (act * up_f).astype(jnp.bfloat16)
    zb, x = lax.axis_index("zb"), lax.axis_index("x")

    part = exchange(jnp.broadcast_to(hidden[None], (4,) + hidden.shape), ("za_hi", "za_lo"))
    pair = in_order(grad_out, swap(grad_out, "zh", 2, 1), lax.axis_index("zh") == 1, 0)
    spread = (jnp.arange(width)[None] // BLOCK == jnp.arange(width // BLOCK)[:, None]).astype(jnp.float32)
    scale = lax.dot_general(weight_scales, spread, (((0,), (0,)), ((), ())), preferred_element_type=jnp.float32)
    weight = (weight_values.astype(jnp.float32) * scale).astype(jnp.bfloat16)
    pair, part, weight = lax.optimization_barrier((pair, part, weight))

    mine = in_order(part, swap(part, "zb", 2, 1), zb == 1, 1).reshape(128, units)
    grads = exchange(jnp.broadcast_to(pair[None], (8,) + pair.shape), ("y", "core"))
    grads = grads.reshape(2, 2, 2, 2, 2, 16, width)
    by_part = grads.transpose(2, 4, 3, 1, 0, 5, 6).reshape(512, width)
    by_x = grads.transpose(2, 4, 0, 1, 3, 5, 6).reshape(4, 128, width)
    partial = lax.dot_general(
        by_part, weight, (((1,), (1,)), ((), ())), preferred_element_type=jnp.float32
    ).astype(jnp.bfloat16)
    partial, mine = lax.optimization_barrier((partial, mine))

    over_x = exchange(partial.reshape(8, 64, units), ("x", "zb"))
    next_x = shift(mine, 3)
    last_x = shift(mine, 1)
    far_x = shift(mine, 2)
    over_x = over_x.astype(jnp.float32).sum(0).astype(jnp.bfloat16)
    over_z = exchange(over_x.reshape(4, 16, units), ("za_lo", "za_hi"))
    hidden_grad = over_z.astype(jnp.float32).sum(0)

    all_hidden = jnp.concatenate([mine, next_x, far_x, last_x])
    rolled = lax.dynamic_slice_in_dim(jnp.concatenate([by_x, by_x]), x, 4).reshape(512, width)
    weight_grad = lax.dot_general(
        all_hidden, rolled, (((0,), (0,)), ((), ())), preferred_element_type=jnp.float32
    ).astype(jnp.bfloat16)
    gate_grad = (hidden_grad * up_f * sig * (1.0 + gate_f * (1.0 - sig))).astype(jnp.bfloat16)
    up_grad = (hidden_grad * act).astype(jnp.bfloat16)
    return (weight_grad, gate_grad, up_grad)


def solution(mesh):
    fine = Mesh(mesh.devices.reshape(4, 2, 2, 2, 2, 2, 4), ("y", "zh", "core", "za_hi", "za_lo", "zb", "x"))
    row, col = ("y", "zh", "core"), ("za_hi", "za_lo", "zb", "x")
    placed = (P(row, col), P(col, row), P(col, row), P(row, col), P(col, row))
    return jax.shard_map(
        per_device,
        mesh=fine,
        in_specs=placed,
        out_specs=(P(row, col), P(col, row), P(col, row)),
        check_vma=False,
    )
```

```python
import jax
import jax.numpy as jnp
from jax import lax
from jax.sharding import Mesh, PartitionSpec as P

BLOCK = 32


def exchange(parts, axes):
    return lax.all_to_all(parts, axes, split_axis=0, concat_axis=0)


def swap(block, axis, size, stride):
    return lax.ppermute(block, axis, [(i, i ^ stride) for i in range(size)])


def shift(block, k):
    return lax.ppermute(block, "x", [(i, (i + k) % 4) for i in range(4)])


def in_order(mine, other, upper, axis):
    return jnp.where(upper, jnp.stack([other, mine], axis), jnp.stack([mine, other], axis))


def per_device(grad_out, gate_pre, up_pre, weight_values, weight_scales):
    units = gate_pre.shape[1]
    width = grad_out.shape[1]
    gate_f = gate_pre.astype(jnp.float32)
    up_f = up_pre.astype(jnp.float32)
    sig = jax.nn.sigmoid(gate_f)
    act = gate_f * sig
    hidden = (act * up_f).astype(jnp.bfloat16)
    zb, x = lax.axis_index("zb"), lax.axis_index("x")

    part = exchange(jnp.broadcast_to(hidden[None], (4,) + hidden.shape), ("za_hi", "za_lo"))
    pair = in_order(grad_out, swap(grad_out, "zh", 2, 1), lax.axis_index("zh") == 1, 0)
    spread = (jnp.arange(width)[None] // BLOCK == jnp.arange(width // BLOCK)[:, None]).astype(jnp.float32)
    scale = lax.dot_general(weight_scales, spread, (((0,), (0,)), ((), ())), preferred_element_type=jnp.float32)
    weight = (weight_values.astype(jnp.float32) * scale).astype(jnp.bfloat16)
    pair, part, weight = lax.optimization_barrier((pair, part, weight))

    mine = in_order(part, swap(part, "zb", 2, 1), zb == 1, 1).reshape(128, units)
    grads = exchange(jnp.broadcast_to(pair[None], (8,) + pair.shape), ("y", "core"))
    grads = grads.reshape(2, 2, 2, 2, 2, 16, width)
    by_part = grads.transpose(2, 4, 3, 1, 0, 5, 6).reshape(512, width)
    by_x = grads.transpose(2, 4, 0, 1, 3, 5, 6).reshape(4, 128, width)
    partial = lax.dot_general(
        by_part, weight, (((1,), (1,)), ((), ())), preferred_element_type=jnp.float32
    ).astype(jnp.bfloat16)
    partial, mine = lax.optimization_barrier((partial, mine))

    over_x = exchange(partial.reshape(8, 64, units), ("x", "zb"))
    next_x = shift(mine, 3)
    last_x = shift(mine, 1)
    far_x = shift(mine, 2)
    over_x = over_x.astype(jnp.float32).sum(0).astype(jnp.bfloat16)
    over_z = exchange(over_x.reshape(4, 16, units), ("za_lo", "za_hi"))
    hidden_grad = over_z.astype(jnp.float32).sum(0)

    all_hidden = jnp.concatenate([mine, far_x, next_x, last_x])
    twice = jnp.concatenate([by_x, by_x])
    rolled = jnp.concatenate([lax.dynamic_slice_in_dim(twice, x + k, 1) for k in (0, 2, 1, 3)]).reshape(512, width)
    weight_grad = lax.dot_general(
        all_hidden, rolled, (((0,), (0,)), ((), ())), preferred_element_type=jnp.float32
    ).astype(jnp.bfloat16)
    gate_grad = (hidden_grad * up_f * sig * (1.0 + gate_f * (1.0 - sig))).astype(jnp.bfloat16)
    up_grad = (hidden_grad * act).astype(jnp.bfloat16)
    return (weight_grad, gate_grad, up_grad)


def solution(mesh):
    fine = Mesh(mesh.devices.reshape(4, 2, 2, 2, 2, 2, 4), ("y", "zh", "core", "za_hi", "za_lo", "zb", "x"))
    row, col = ("y", "zh", "core"), ("za_hi", "za_lo", "zb", "x")
    placed = (P(row, col), P(col, row), P(col, row), P(row, col), P(col, row))
    return jax.shard_map(
        per_device,
        mesh=fine,
        in_specs=placed,
        out_specs=(P(row, col), P(col, row), P(col, row)),
        check_vma=False,
    )
```

```python
import jax
import jax.numpy as jnp
from jax import lax
from jax.sharding import Mesh, PartitionSpec as P

BLOCK = 32


def exchange(parts, axes):
    return lax.all_to_all(parts, axes, split_axis=0, concat_axis=0)


def swap(block, axis, size, stride):
    return lax.ppermute(block, axis, [(i, i ^ stride) for i in range(size)])


def in_order(mine, other, upper, axis):
    return jnp.where(upper, jnp.stack([other, mine], axis), jnp.stack([mine, other], axis))


def per_device(grad_out, gate_pre, up_pre, weight_values, weight_scales):
    units = gate_pre.shape[1]
    width = grad_out.shape[1]
    gate_f = gate_pre.astype(jnp.float32)
    up_f = up_pre.astype(jnp.float32)
    sig = jax.nn.sigmoid(gate_f)
    act = gate_f * sig
    hidden = (act * up_f).astype(jnp.bfloat16)
    zb, x = lax.axis_index("zb"), lax.axis_index("x")

    part = exchange(jnp.broadcast_to(hidden[None], (4,) + hidden.shape), "za")
    pair = in_order(grad_out, swap(grad_out, "zh", 2, 1), lax.axis_index("zh") == 1, 0)
    spread = (jnp.arange(width)[None] // BLOCK == jnp.arange(width // BLOCK)[:, None]).astype(jnp.float32)
    scale = lax.dot_general(weight_scales, spread, (((0,), (0,)), ((), ())), preferred_element_type=jnp.float32)
    weight = (weight_values.astype(jnp.float32) * scale).astype(jnp.bfloat16)
    pair, part, weight = lax.optimization_barrier((pair, part, weight))

    mine = in_order(part, swap(part, "zb", 2, 1), zb == 1, 1).reshape(128, units)
    grads = exchange(jnp.broadcast_to(pair[None], (8,) + pair.shape), ("y", "core"))
    grads = grads.reshape(4, 2, 2, 2, 16, width)
    by_part = grads.transpose(1, 3, 2, 0, 4, 5).reshape(512, width)
    by_x = grads.transpose(1, 3, 0, 2, 4, 5).reshape(4, 128, width)
    partial = lax.dot_general(
        by_part, weight, (((1,), (1,)), ((), ())), preferred_element_type=jnp.float32
    ).astype(jnp.bfloat16)
    partial, mine = lax.optimization_barrier((partial, mine))

    over_x = exchange(partial.reshape(8, 64, units), ("x", "zb"))
    near_x, far_x, around_x = [swap(mine, "x", 4, k) for k in (1, 2, 3)]
    over_x = over_x.astype(jnp.float32).sum(0).astype(jnp.bfloat16)
    over_z = exchange(over_x.reshape(4, 16, units), "za")
    hidden_grad = over_z.astype(jnp.float32).sum(0)

    all_hidden = jnp.concatenate([mine, far_x, around_x, near_x])
    rolled = jnp.concatenate([lax.dynamic_slice_in_dim(by_x, x ^ k, 1) for k in (0, 2, 3, 1)]).reshape(512, width)
    weight_grad = lax.dot_general(
        all_hidden, rolled, (((0,), (0,)), ((), ())), preferred_element_type=jnp.float32
    ).astype(jnp.bfloat16)
    gate_grad = (hidden_grad * up_f * sig * (1.0 + gate_f * (1.0 - sig))).astype(jnp.bfloat16)
    up_grad = (hidden_grad * act).astype(jnp.bfloat16)
    return (weight_grad, gate_grad, up_grad)


def solution(mesh):
    fine = Mesh(mesh.devices.reshape(4, 2, 2, 4, 2, 4), ("y", "zh", "core", "za", "zb", "x"))
    row, col = ("y", "zh", "core"), ("za", "zb", "x")
    placed = (P(row, col), P(col, row), P(col, row), P(row, col), P(col, row))
    return jax.shard_map(
        per_device,
        mesh=fine,
        in_specs=placed,
        out_specs=(P(row, col), P(col, row), P(col, row)),
        check_vma=False,
    )
```
